256 devices in a mesh: helper: 32 (over x_lo, z, core), tensor: 8 (over y, x_hi).
Axes of the slice: x: 4 (x_hi: 2, x_lo: 2; x = x_hi * 2 + x_lo), y: 4, z: 8, core: 2. Of those that a mesh axis runs over, the one named last changes fastest.
Arguments:
- recorded_input_rows: bfloat16 [32768, 2048], P('helper'), may hold values from -12 to 12
- out_cotangent: bfloat16 [32768, 2048], P('helper'), may hold values from -1.25 to 1.25
- fresh_rows: bfloat16 [8192, 2048], P('helper'), may hold values from -6 to 6
- seq_counts: int32 [32], replicated, may hold values from 1 to 4, 48 in all
- decay_logs: float32 [16, 256], P('tensor'), may hold values from -3 to 0
- norm_gain: float32 [2048], P('tensor'), may hold values from 0.25 to 1.75
- qkv_weight: float32 [2048, 3, 2048], P('helper', None, 'tensor'), may hold values from -0.125 to 0.125
- emitted_projection_matrix: float32 [2048, 2048], P('helper', 'tensor'), may hold values from -0.125 to 0.125
- qkv_first: float32 [2048, 3, 2048], P('helper', None, 'tensor'), may hold values from -6 to 6
- qkv_second: float32 [2048, 3, 2048], P('helper', None, 'tensor'), may hold values from 1 to 100
- out_first: float32 [2048, 2048], P('helper', 'tensor'), may hold values from -6 to 6
- out_second: float32 [2048, 2048], P('helper', 'tensor'), may hold values from 1 to 100
Outputs:
- fresh_out: bfloat16 [8192, 2048], P('helper')
- qkv_moment: float32 [2048, 3, 2048], P('helper', None, 'tensor')
- out_moment: float32 [2048, 2048], P('helper', 'tensor')
The draws below stay inside these ranges and needn't reach their ends.
Inputs may be any that keep to these rules, and one draw needn't show every extreme that they name: Helper h's live sequences are its first seq_counts[h] slots; the counts sum to three halves of the number of helpers, and the largest equals 4.
All inputs are finite; a program needn't handle non-finite values.
Results may differ from the reference program's by a relative error of at most 0.0095.
The reference program's roundings to bfloat16 on the way count: a program that leaves them out, or rounds other values in their place, can miss the bound.
Values may be sent and summed in bfloat16 or wider, within the bound.
No kernel may reach another device: no remote copies, remote signals or barrier semaphores. Data moves between devices by JAX's collectives and lax.ppermute only.
A program may use at most 128 MiB of HBM per device.

```python
import math
import jax
import jax.numpy as jnp
import numpy as np
from jax import lax

HEADS = 16
D = 2048
SEQ_LEN = 256
SEQ_CAP = 4
N_HELPER = 32


def draw_decay_logs(key, part):
    key_rate = jax.random.fold_in(key, 11)
    key_place = jax.random.fold_in(key, 12)
    key_loss = jax.random.fold_in(key, 13)
    low_log = jnp.log(0.1 / SEQ_LEN)
    high_log = jnp.log(1.0 / 30.0)
    channel_fading_multiplier = jnp.exp(jax.random.uniform(key_rate, (HEADS, 1), jnp.float32, low_log, high_log))
    bucket_addresses = jax.random.randint(key_place, (HEADS, 3), 0, SEQ_LEN)
    objective_readings = jax.random.uniform(key_loss, (HEADS, 3), jnp.float32, 0.2, 0.5)
    element_indices = jnp.arange(SEQ_LEN)
    run_extent_list = jnp.sum(jnp.where(element_indices[None, None, :] == bucket_addresses[:, :, None], jnp.log(1.0 - objective_readings)[:, :, None], 0.0), axis=1)
    return (run_extent_list - channel_fading_multiplier).astype(jnp.float32)


def with_spikes(drawn, rng, source, target, parts, factor):
    owner, partner = [(jnp.arange(drawn.shape[position]) // (drawn.shape[position] // parts)).reshape([-1 if axis == position else 1 for axis in range(drawn.ndim)]) for position in (source, target)]
    chosen = jax.random.permutation(rng, parts)[partner]
    strong = (owner == chosen) | (owner == (partner + parts // 2) % parts)
    return jnp.where(strong, factor * drawn, drawn)


def shard_levels(stream_key, shape, cuts, smallest, high):
    gain = 1.0
    for dim, blocks in cuts:
        steps = jax.random.uniform(jax.random.fold_in(jax.random.fold_in(stream_key, 6), dim), (blocks,), jnp.float32, smallest / len(cuts), high / len(cuts))
        gain = gain * jnp.repeat(jnp.exp(steps), shape[dim] // blocks).reshape((-1,) + (1,) * (len(shape) - 1 - dim))
    return gain


def profile(count, total, bound, lean):
    loads = [(1 << 20) // math.isqrt(rank ** lean) + 1 for rank in range(2, count + 1)]
    rest, given = total - bound - (count - 1), [1] * (count - 1)
    while rest > 0:
        movable = [i for i in range(count - 1) if given[i] < bound]
        pool, left = sum([loads[i] for i in movable]), rest
        for i in movable:
            extra = min(bound - given[i], max(1, left * loads[i] // pool), rest)
            given[i] = given[i] + extra
            rest = rest - extra
    return np.array([bound] + given)


def uneven_parts(rng, count, total, limit, skew):
    if count == 2:
        one = jax.random.randint(rng, (), max(1, total - limit), min(limit, total - 1) + 1)
        return jnp.stack([one, total - one])
    sizes = jnp.asarray(profile(count, total, limit, skew), jnp.int32)
    twos = (count - 1) // 2
    donor, receiver = sizes[1:1 + 2 * twos:2], sizes[2:2 + 2 * twos:2]
    margin = jnp.minimum(donor - 1, limit - receiver)
    moved = jax.random.randint(jax.random.fold_in(rng, 1), (twos,), 0, 1 << 20) % (margin + 1)
    sizes = sizes.at[1:1 + 2 * twos:2].set(donor - moved).at[2:2 + 2 * twos:2].set(receiver + moved)
    return sizes[jax.random.permutation(jax.random.fold_in(rng, 2), count)]


def scatter_about(stream_key, extent, deviation, bound, cuts=(), kind=jnp.bfloat16):
    result = deviation * jax.random.normal(stream_key, extent, jnp.float32)
    if cuts:
        result = result * shard_levels(stream_key, extent, cuts, -0.22, 0.18)
    return jnp.clip(result, -bound, bound).astype(kind)


def heavy_noise(stream_key, shape, deviation, reach, shards, heavy, held_as=jnp.bfloat16):
    values = deviation * jax.random.normal(stream_key, shape, jnp.float32)
    if shards:
        values = values * shard_levels(stream_key, shape, shards, -0.22, 0.18)
    return jnp.clip(with_spikes(values, jax.random.fold_in(stream_key, 3), *heavy), -reach, reach).astype(held_as)


def setup_inputs(seed: int = 0) -> dict:
    key_list = jax.random.split(jax.random.key(seed), 13)
    recorded_input_rows = heavy_noise(key_list[0], (N_HELPER * SEQ_CAP * SEQ_LEN, D), 1.0, 12.0, ((0, 32),), (0, 1, 32, 2.75))
    out_cotangent = heavy_noise(key_list[1], (N_HELPER * SEQ_CAP * SEQ_LEN, D), 0.1, 1.25, ((0, 32),), (0, 1, 32, 2.75))
    fresh_rows = scatter_about(key_list[2], (N_HELPER * SEQ_LEN, D), 1.0, 6.0, ((0, 32),))
    seq_counts = uneven_parts(key_list[3], N_HELPER, 3 * N_HELPER // 2, SEQ_CAP, 2).astype(jnp.int32)
    decay_logs = draw_decay_logs(jax.random.fold_in(key_list[12], 71), 0)
    norm_gain = jnp.clip(1.0 + 0.15 * jax.random.normal(key_list[5], (D,), jnp.float32), 0.25, 1.75)
    qkv_weight = scatter_about(key_list[6], (D, 3, D), D ** -0.5, 0.125, ((0, 32), (2, 8)), jnp.float32)
    emitted_projection_matrix = scatter_about(key_list[7], (D, D), D ** -0.5, 0.125, ((0, 32), (1, 8)), jnp.float32)
    qkv_first = scatter_about(key_list[8], (D, 3, D), 1.0, 6.0, ((0, 32), (2, 8)), jnp.float32)
    qkv_second = jnp.clip(jnp.exp(math.log(100.0) - 4.6051702 * jax.random.uniform(key_list[9], (D, 3, D), jnp.float32) ** shard_levels(key_list[9], (D, 3, D), ((0, 32), (2, 8)), -0.2, 0.2)), 1.0, 100.0)
    out_first = scatter_about(key_list[10], (D, D), 1.0, 6.0, ((0, 32), (1, 8)), jnp.float32)
    out_second = jnp.clip(jnp.exp(math.log(100.0) - 4.6051702 * jax.random.uniform(key_list[11], (D, D), jnp.float32) ** shard_levels(key_list[11], (D, D), ((0, 32), (1, 8)), -0.2, 0.2)), 1.0, 100.0)
    return dict(recorded_input_rows=recorded_input_rows, out_cotangent=out_cotangent, fresh_rows=fresh_rows, seq_counts=seq_counts, decay_logs=decay_logs, norm_gain=norm_gain, qkv_weight=qkv_weight, emitted_projection_matrix=emitted_projection_matrix, qkv_first=qkv_first, qkv_second=qkv_second, out_first=out_first, out_second=out_second)


NORM_FLOOR = 1.0
BETA_ONE = 0.9
BETA_TWO = 0.95
ADAM_EPS = 1e-08
LEARN_RATE = 0.005
WEIGHT_DECAY = 0.1
BIAS_ONE = 0.9999734386011124
BIAS_TWO = 0.994079470779666

def product_of(form, left, right):
    return jnp.einsum(form, left.astype(jnp.float32), right.astype(jnp.float32))

def decay_table(decay_logs):
    running = jnp.cumsum(decay_logs.astype(jnp.float32), axis=1)
    length = decay_logs.shape[1]
    later = (jnp.arange(length)[:, None] >= jnp.arange(length)[None, :])[None]
    spread_factor = running[:, :, None] - running[:, None, :]
    return jnp.where(later, jnp.exp(jnp.where(later, spread_factor, 0.0)), 0.0)

def attend(projected, decay_mask, norm_gain):
    head_count = decay_mask.shape[0]
    split_shape = (projected.shape[0], projected.shape[1], head_count, projected.shape[3] // head_count)
    raw_query = projected[:, :, 0].reshape(split_shape)
    raw_key = projected[:, :, 1].reshape(split_shape)
    queries = (raw_query * jax.nn.sigmoid(raw_query)).astype(jnp.bfloat16)
    key_rows = (raw_key * jax.nn.sigmoid(raw_key)).astype(jnp.bfloat16)
    values = projected[:, :, 2].reshape(split_shape).astype(jnp.bfloat16)
    scores = product_of('sthd,suhd->shtu', queries, key_rows)
    weights = (scores * decay_mask[None]).astype(jnp.bfloat16)
    mixed = product_of('shtu,suhd->sthd', weights, values)
    mean_square = lax.optimization_barrier(jnp.mean(mixed * mixed, axis=-1, keepdims=True))
    active = jnp.where(mean_square > NORM_FLOOR, 1.0, 0.0)
    inverse = lax.rsqrt(jnp.maximum(mean_square, NORM_FLOOR))
    gain_heads = norm_gain.reshape(head_count, -1)
    attended = (mixed * inverse * gain_heads).astype(jnp.bfloat16)
    return (attended, (raw_query, raw_key, queries, key_rows, values, weights, mixed, inverse, active))

def attend_back(grad_attended, stashed, decay_mask, norm_gain):
    raw_query, raw_key, queries, key_rows, values, weights, mixed, inverse, active = stashed
    gain_heads = norm_gain.reshape(decay_mask.shape[0], -1)
    scaled = grad_attended * gain_heads
    grad_mixed = inverse * scaled - active * mixed * (inverse * inverse * inverse) * lax.optimization_barrier(jnp.mean(scaled * mixed, axis=-1, keepdims=True))
    grad_mixed = grad_mixed.astype(jnp.bfloat16)
    grad_weights = product_of('sthd,suhd->shtu', grad_mixed, values)
    grad_values = product_of('shtu,sthd->suhd', weights, grad_mixed)
    grad_scores = (grad_weights * decay_mask[None]).astype(jnp.bfloat16)
    grad_query = product_of('shtu,suhd->sthd', grad_scores, key_rows)
    grad_key = product_of('shtu,sthd->suhd', grad_scores, queries)
    sigma_query = jax.nn.sigmoid(raw_query)
    sigma_key = jax.nn.sigmoid(raw_key)
    grad_query = grad_query * sigma_query * (1.0 + raw_query * (1.0 - sigma_query))
    grad_key = grad_key * sigma_key * (1.0 + raw_key * (1.0 - sigma_key))
    return jnp.stack([grad_query, grad_key, grad_values], axis=2)

def adam_step(weight, first_moment, second_moment, gradient):
    first_new = BETA_ONE * first_moment + (1.0 - BETA_ONE) * gradient
    second_new = BETA_TWO * second_moment + (1.0 - BETA_TWO) * gradient * gradient
    update = first_new / BIAS_ONE / (jnp.sqrt(second_new / BIAS_TWO) + ADAM_EPS)
    weight_new = weight - LEARN_RATE * (update + WEIGHT_DECAY * weight)
    return (weight_new.astype(jnp.bfloat16), first_new)

def reference(recorded_input_rows, out_cotangent, fresh_rows, seq_counts, decay_logs, norm_gain, qkv_weight, emitted_projection_matrix, qkv_first, qkv_second, out_first, out_second):
    decay_mask = decay_table(decay_logs)
    model_width = qkv_weight.shape[0]
    head_count = decay_logs.shape[0]
    slot_total = recorded_input_rows.shape[0] // SEQ_LEN
    old_qkv = qkv_weight.astype(jnp.bfloat16).reshape(model_width, 3 * model_width)
    old_out = emitted_projection_matrix.astype(jnp.bfloat16)
    slot_index = (jnp.arange(slot_total) % SEQ_CAP).astype(jnp.int32)
    slot_limit = jnp.repeat(seq_counts.astype(jnp.int32), SEQ_CAP)
    slot_live = (slot_index < slot_limit).astype(jnp.float32)
    logged_seqs = recorded_input_rows.reshape(slot_total, SEQ_LEN, model_width)
    cot_seqs = out_cotangent.reshape(slot_total, SEQ_LEN, model_width)

    def replay_one(totals, inputs):
        seq_rows, seq_cot, live_flag = inputs

        def live_branch(partial_sums):
            projected = jnp.dot(seq_rows, old_qkv, preferred_element_type=jnp.float32).reshape(1, SEQ_LEN, 3, model_width)
            attended, stashed = attend(projected, decay_mask, norm_gain)
            grad_attended = jnp.dot(seq_cot, old_out, preferred_element_type=jnp.float32).reshape(1, SEQ_LEN, head_count, -1)
            grad_projected = attend_back(grad_attended, stashed, decay_mask, norm_gain)
            grad_projected = grad_projected.reshape(SEQ_LEN, 3 * model_width).astype(jnp.bfloat16)
            qkv_sum = partial_sums[0] + jnp.dot(seq_rows.T, grad_projected, preferred_element_type=jnp.float32)
            out_sum = partial_sums[1] + jnp.dot(seq_cot.T, attended.reshape(SEQ_LEN, model_width), preferred_element_type=jnp.float32)
            return (qkv_sum, out_sum)

        def inactive_branch(partial_sums):
            return partial_sums
        return (lax.cond(live_flag > 0.5, live_branch, inactive_branch, totals), None)
    start_sums = (jnp.zeros((model_width, 3 * model_width), jnp.float32), jnp.zeros((model_width, model_width), jnp.float32))
    prefix_accumulated = lax.scan(replay_one, start_sums, (logged_seqs, cot_seqs, slot_live))
    qkv_grad, out_grad = prefix_accumulated[0]
    new_qkv, qkv_moment = adam_step(qkv_weight, qkv_first, qkv_second, qkv_grad.reshape(model_width, 3, model_width))
    new_out, out_moment = adam_step(emitted_projection_matrix, out_first, out_second, out_grad)
    fresh_qkv = new_qkv.reshape(model_width, 3 * model_width)

    def recomputed_single(seq_rows):
        projected = jnp.dot(seq_rows, fresh_qkv, preferred_element_type=jnp.float32).reshape(1, SEQ_LEN, 3, model_width)
        attended = attend(projected, decay_mask, norm_gain)[0].reshape(SEQ_LEN, model_width)
        summed = seq_rows.astype(jnp.float32) + jnp.dot(attended, new_out.T, preferred_element_type=jnp.float32)
        return summed.astype(jnp.bfloat16)
    fresh_out = lax.map(recomputed_single, fresh_rows.reshape(-1, SEQ_LEN, model_width)).reshape(-1, model_width)
    return (fresh_out, qkv_moment, out_moment)
```

```python
import functools

import jax
import jax.numpy as jnp
from jax import lax
from jax.experimental import pallas as pl
from jax.experimental.pallas import tpu as pltpu
from jax.sharding import PartitionSpec as P

SEQ_LEN = 256
HEAD = 128

NORM_FLOOR = 1.0
BETA_ONE = 0.9
BETA_TWO = 0.95
ADAM_EPS = 1e-08
LEARN_RATE = 0.005
WEIGHT_DECAY = 0.1
BIAS_ONE = 0.9999734386011124
BIAS_TWO = 0.994079470779666

NX, NZ, NC = 2, 8, 2
NH = NX * NZ * NC
F32, BF16 = jnp.float32, jnp.bfloat16
VMEM = pl.BlockSpec(memory_space=pltpu.VMEM)
SMEM = pl.BlockSpec(memory_space=pltpu.SMEM)


def helper_of(x, z, c):
    return (x * NZ + z) * NC + c


def helper_move(block, dx, dz, dc):
    pairs = [
        (helper_of((x + dx) % NX, (z + dz) % NZ, (c + dc) % NC), helper_of(x, z, c))
        for x in range(NX)
        for z in range(NZ)
        for c in range(NC)
    ]
    return lax.ppermute(block, "helper", pairs)


def tensor_move(block, shift, count):
    return lax.ppermute(
        block, "tensor", [((i + shift) % count, i) for i in range(count)]
    )


def decay_table(decay_logs):
    length = decay_logs.shape[1]
    later = (jnp.arange(length)[:, None] >= jnp.arange(length)[None, :])[None]
    running = jnp.sum(jnp.where(later, decay_logs[:, None, :], 0.0), axis=2)
    spread_factor = running[:, :, None] - running[:, None, :]
    return jnp.where(later, jnp.exp(jnp.where(later, spread_factor, 0.0)), 0.0)


def dot(a, b, ca, cb):
    return lax.dot_general(a, b, (((ca,), (cb,)), ((), ())), preferred_element_type=F32)


def gather_pieces(piece):
    near = [piece] + [helper_move(piece, 0, k, 0) for k in range(1, NZ)]
    both = near + [helper_move(p, 1, 0, 0) for p in near]
    return both + [helper_move(p, 0, 0, 1) for p in both]


def place(pieces, where_ref, full):
    x, z, c = where_ref[1], where_ref[2], where_ref[3]
    rows = pieces[0].shape[1]
    for index, piece in enumerate(pieces):
        dc, dx, dz = index // (NX * NZ), index // NZ % NX, index % NZ
        owner = helper_of((x + dx) % NX, (z + dz) % NZ, (c + dc) % NC)
        start = pl.multiple_of(owner * rows, rows)
        for m in range(piece.shape[0]):
            full[m, pl.ds(start, rows), :] = piece[m]


def head_forward(raw_query, raw_key, raw_value, mask, gain):
    sigma_query, sigma_key = jax.nn.sigmoid(raw_query), jax.nn.sigmoid(raw_key)
    queries = (raw_query * sigma_query).astype(BF16)
    key_rows = (raw_key * sigma_key).astype(BF16)
    values = raw_value.astype(BF16)
    weights = (dot(queries, key_rows, 1, 1) * mask).astype(BF16)
    mixed = dot(weights, values, 1, 0)
    mean_square = jnp.mean(mixed * mixed, axis=-1, keepdims=True)
    inverse = lax.rsqrt(jnp.maximum(mean_square, NORM_FLOOR))
    attended = (mixed * inverse * gain).astype(BF16)
    return attended, (sigma_query, sigma_key, queries, key_rows, values, weights, mixed, mean_square, inverse)


def replay_kernel(where_ref, x_ref, cot_ref, xt_ref, cott_ref, mask_ref, gain_ref, *refs):
    pieces, (out_ref, full, grad_p, att) = refs[:NH], refs[NH:]
    place(pieces, where_ref, full)
    live = where_ref[0]
    slots = x_ref.shape[0] // SEQ_LEN
    for s in range(slots):
        rows = slice(s * SEQ_LEN, (s + 1) * SEQ_LEN)

        @pl.when(s >= live)
        def _():
            grad_p[rows, :] = jnp.zeros((SEQ_LEN, grad_p.shape[1]), BF16)
            att[rows, :] = jnp.zeros((SEQ_LEN, att.shape[1]), BF16)

        @pl.when(s < live)
        def _():
            seq, cot = x_ref[rows, :], cot_ref[rows, :]
            raw = [dot(seq, full[m], 1, 0) for m in range(3)]
            grad_attended = dot(cot, full[3], 1, 0)
            width = att.shape[1]
            for n in range(width // HEAD):
                cols = slice(n * HEAD, (n + 1) * HEAD)
                mask, gain = mask_ref[n], gain_ref[:, cols]
                raw_query, raw_key = raw[0][:, cols], raw[1][:, cols]
                attended, kept = head_forward(raw_query, raw_key, raw[2][:, cols], mask, gain)
                sigma_query, sigma_key, queries, key_rows, values, weights, mixed, mean_square, inverse = kept
                att[rows, cols] = attended
                scaled = grad_attended[:, cols] * gain
                active = jnp.where(mean_square > NORM_FLOOR, 1.0, 0.0)
                mean_dot = jnp.mean(scaled * mixed, axis=-1, keepdims=True)
                grad_mixed = inverse * scaled - mixed * (active * (inverse * inverse * inverse) * mean_dot)
                grad_mixed = grad_mixed.astype(BF16)
                grad_scores = (dot(grad_mixed, values, 1, 1) * mask).astype(BF16)
                grad_values = dot(weights, grad_mixed, 0, 0)
                grad_query = dot(grad_scores, key_rows, 1, 0)
                grad_key = dot(grad_scores, queries, 0, 0)
                grad_query = grad_query * sigma_query * (1.0 + raw_query * (1.0 - sigma_query))
                grad_key = grad_key * sigma_key * (1.0 + raw_key * (1.0 - sigma_key))
                for m, grad in enumerate((grad_query, grad_key, grad_values)):
                    grad_p[rows, m * width + n * HEAD : m * width + (n + 1) * HEAD] = grad.astype(BF16)
    x, z, c = where_ref[1], where_ref[2], where_ref[3]
    width = att.shape[1]
    shard = out_ref.shape[4]
    chunk = 4 * shard
    for first in range(0, xt_ref.shape[0], chunk):
        qkv = dot(xt_ref[first : first + chunk, :], grad_p[...], 1, 0).astype(BF16)
        out = dot(cott_ref[first : first + chunk, :], att[...], 1, 0).astype(BF16)
        for part in range(chunk // shard):
            owner = first // shard + part
            ox, oz, oc = owner // (NZ * NC), owner // NC % NZ, owner % NC
            rows = slice(part * shard, (part + 1) * shard)
            place_at = ((oc + c) % NC, (ox + x) % NX, (oz + NZ - z) % NZ)
            for m in range(3):
                out_ref[(*place_at, m)] = qkv[rows, m * width : (m + 1) * width]
            out_ref[(*place_at, 3)] = out[rows, :]


def fresh_kernel(where_ref, x_ref, mask_ref, gain_ref, *refs):
    pieces, (out_ref, full, att) = refs[:NH], refs[NH:]
    place(pieces, where_ref, full)
    seq = x_ref[...]
    raw = [dot(seq, full[m], 1, 0) for m in range(3)]
    width = att.shape[1]
    for n in range(width // HEAD):
        cols = slice(n * HEAD, (n + 1) * HEAD)
        att[:, cols] = head_forward(raw[0][:, cols], raw[1][:, cols], raw[2][:, cols], mask_ref[n], gain_ref[:, cols])[0]
    ranks, rows = out_ref.shape[:2]
    mine = where_ref[4]
    for first in range(0, full.shape[1], SEQ_LEN):
        cols = slice(first, first + SEQ_LEN)
        term = dot(att[...], full[3, cols, :], 1, 1).astype(BF16)
        for owner in range(ranks):
            out_ref[(owner + ranks - mine) % ranks, :, cols] = term[owner * rows : (owner + 1) * rows, :]


def order_kernel(where_ref, *refs):
    pieces, out_ref = refs[:-1], refs[-1]
    ranks, rows = len(pieces), pieces[0].shape[0]
    mine = where_ref[4]
    for shift, piece in enumerate(pieces):
        start = pl.multiple_of((mine + shift) % ranks * rows, rows)
        out_ref[pl.ds(start, rows), :] = piece[...]


def kernel_call(body, out_shape, n_vmem, scratch, limit):
    return pl.pallas_call(
        body,
        out_shape=out_shape,
        in_specs=[SMEM] + [VMEM] * n_vmem,
        out_specs=VMEM,
        scratch_shapes=scratch,
        compiler_params=pltpu.CompilerParams(vmem_limit_bytes=limit),
    )


def adam_step(weight, first_moment, second_moment, gradient):
    first_new = BETA_ONE * first_moment + (1.0 - BETA_ONE) * gradient
    second_new = BETA_TWO * second_moment + (1.0 - BETA_TWO) * gradient * gradient
    update = first_new / BIAS_ONE / (jnp.sqrt(second_new / BIAS_TWO) + ADAM_EPS)
    weight_new = weight - LEARN_RATE * (update + WEIGHT_DECAY * weight)
    return (weight_new.astype(BF16), first_new)


def scatter_sum(terms):
    other_core = helper_move(terms[1], 0, 0, 1)
    total = None
    for k in [4, 3, 5, 2, 6, 1, 7, 0]:
        here = [(terms[0, d, k].astype(F32) + other_core[d, k].astype(F32)) for d in range(NX)]
        from_x = helper_move(here[1].astype(BF16), 1, 0, 0)
        block = here[0] + from_x.astype(F32)
        if k:
            block = helper_move(block.astype(BF16), 0, -k, 0).astype(F32)
        total = block if total is None else total + block
    return total


def local(
    recorded_input_rows,
    out_cotangent,
    fresh_rows,
    seq_counts,
    decay_logs,
    norm_gain,
    qkv_weight,
    emitted_projection_matrix,
    qkv_first,
    qkv_second,
    out_first,
    out_second,
):
    shard, _, width = qkv_weight.shape
    depth = shard * NH
    ranks = lax.axis_size("tensor")
    rank = lax.axis_index("tensor")
    here = lax.axis_index("helper")
    live = lax.dynamic_slice(seq_counts, (here,), (1,))[0]
    where = jnp.stack([live, here // (NZ * NC), here // NC % NZ, here % NC, rank]).astype(jnp.int32)
    mask = decay_table(decay_logs)
    gain = norm_gain[None, :]

    def stacked(qkv, out):
        return jnp.concatenate([jnp.transpose(qkv, (1, 0, 2)), out[None]], axis=0)

    old = gather_pieces(stacked(qkv_weight, emitted_projection_matrix).astype(BF16))
    rows = recorded_input_rows.shape[0]
    terms = kernel_call(
        replay_kernel,
        jax.ShapeDtypeStruct((NC, NX, NZ, 4, shard, width), BF16),
        6 + NH,
        [
            pltpu.VMEM((4, depth, width), BF16),
            pltpu.VMEM((rows, 3 * width), BF16),
            pltpu.VMEM((rows, width), BF16),
        ],
        56 * 2**20,
    )(
        where,
        recorded_input_rows,
        out_cotangent,
        recorded_input_rows.T,
        out_cotangent.T,
        mask,
        gain,
        *old,
    )
    grad = scatter_sum(terms)
    new_qkv, qkv_moment = adam_step(qkv_weight, qkv_first, qkv_second, jnp.transpose(grad[:3], (1, 0, 2)))
    new_out, out_moment = adam_step(emitted_projection_matrix, out_first, out_second, grad[3])
    new = gather_pieces(stacked(new_qkv, new_out))
    part = fresh_rows.shape[0] // ranks
    partial = kernel_call(
        fresh_kernel,
        jax.ShapeDtypeStruct((ranks, part, depth), BF16),
        3 + NH,
        [pltpu.VMEM((4, depth, width), BF16), pltpu.VMEM((fresh_rows.shape[0], width), BF16)],
        40 * 2**20,
    )(where, fresh_rows, mask, gain, *new)
    total = lax.dynamic_slice(fresh_rows, (rank * part, 0), (part, depth)).astype(F32) + partial[0].astype(F32)
    for k in range(1, ranks):
        total = total + tensor_move(partial[k], -k, ranks).astype(F32)
    mine = total.astype(BF16)
    blocks = [mine] + [tensor_move(mine, k, ranks) for k in range(1, ranks)]
    fresh_out = kernel_call(
        order_kernel, jax.ShapeDtypeStruct(fresh_rows.shape, BF16), ranks, [], 16 * 2**20
    )(where, *blocks)
    return (fresh_out, qkv_moment, out_moment)


def solution(mesh):
    return jax.shard_map(
        local,
        mesh=mesh,
        in_specs=(
            P("helper", None),
            P("helper", None),
            P("helper", None),
            P(),
            P("tensor", None),
            P("tensor"),
            P("helper", None, "tensor"),
            P("helper", "tensor"),
            P("helper", None, "tensor"),
            P("helper", None, "tensor"),
            P("helper", "tensor"),
            P("helper", "tensor"),
        ),
        out_specs=(P("helper", None), P("helper", None, "tensor"), P("helper", "tensor")),
        check_vma=False,
    )
```

```python
import functools

import jax
import jax.numpy as jnp
from jax import lax
from jax.experimental import pallas as pl
from jax.experimental.pallas import tpu as pltpu
from jax.sharding import PartitionSpec as P

SEQ_LEN = 256
HEAD = 128

NORM_FLOOR = 1.0
BETA_ONE = 0.9
BETA_TWO = 0.95
ADAM_EPS = 1e-08
LEARN_RATE = 0.005
WEIGHT_DECAY = 0.1
BIAS_ONE = 0.9999734386011124
BIAS_TWO = 0.994079470779666

CORE, X_LO, NZ = 1, 16, 8
SETS = ((0, 1), (-1, -2), (2, 3), (-3, -4))
NH = 32
F32, BF16 = jnp.float32, jnp.bfloat16
VMEM = pl.BlockSpec(memory_space=pltpu.VMEM)
SMEM = pl.BlockSpec(memory_space=pltpu.SMEM)


def swap(block, distance):
    return lax.ppermute(block, "helper", [(i ^ distance, i) for i in range(NH)])


def z_swap(block, step):
    def partner(i):
        x, z, c = i // (2 * NZ), i // 2 % NZ, i % 2
        return (x * NZ + (z + (1 if (z + c + step) % 2 == 0 else -1)) % NZ) * 2 + c

    return lax.ppermute(block, "helper", [(partner(i), i) for i in range(NH)])


def z_owner(z, distance, side):
    sign = (1 - 2 * (z % 2)) * (1 - 2 * side)
    return (z + sign * distance + NZ) % NZ


def decay_table(decay_logs):
    length = decay_logs.shape[1]
    later = (jnp.arange(length)[:, None] >= jnp.arange(length)[None, :])[None]
    running = jnp.sum(jnp.where(later, decay_logs[:, None, :], 0.0), axis=2)
    spread_factor = running[:, :, None] - running[:, None, :]
    return jnp.where(later, jnp.exp(jnp.where(later, spread_factor, 0.0)), 0.0)


def dot(a, b, ca, cb):
    return lax.dot_general(a, b, (((ca,), (cb,)), ((), ())), preferred_element_type=F32)


def side_of(parts, first_core, own):
    return jnp.where(first_core == own, parts[:2], parts[2:])


def gather_pieces(piece, first_core):
    mine, theirs = side_of(piece, first_core, True), swap(side_of(piece, first_core, False), CORE)
    rows = [jnp.where(first_core, mine, theirs), jnp.where(first_core, theirs, mine)]
    block = jnp.concatenate(rows, axis=1)[None]
    got, other_x = [block], []
    for step in range(4):
        other_x.append(swap(got[-1], X_LO))
        now = z_swap(block, step)
        now, other_x[-1] = lax.optimization_barrier((now, other_x[-1]))
        got.append(now)
        block = now if step else jnp.concatenate([block, now])
    got = got + other_x + [swap(got[-1], X_LO)]
    return got + [swap(block, CORE) for block in got]


PIECES = [(c, x, z) for c in range(2) for x in range(2) for z in (SETS[0][:1], SETS[0][1:], *SETS[1:])]


def place(pieces, here, full):
    z = here // 2 % NZ
    parts, rows = pieces[0].shape[1:3]
    for (c, x, distances), piece in zip(PIECES, pieces):
        side = here % 2 ^ c
        for block, distance in enumerate(distances):
            owner = (here // (2 * NZ) ^ x) * NZ + z_owner(z, distance, side)
            start = pl.multiple_of(owner * rows, rows)
            for m in range(parts):
                full[side * parts + m, pl.ds(start, rows), :] = piece[block, m]


def head_forward(raw_query, raw_key, raw_value, mask, gain):
    sigma_query, sigma_key = jax.nn.sigmoid(raw_query), jax.nn.sigmoid(raw_key)
    queries = (raw_query * sigma_query).astype(BF16)
    key_rows = (raw_key * sigma_key).astype(BF16)
    values = raw_value.astype(BF16)
    weights = (dot(queries, key_rows, 1, 1) * mask).astype(BF16)
    mixed = dot(weights, values, 1, 0)
    mean_square = jnp.mean(mixed * mixed, axis=-1, keepdims=True)
    inverse = lax.rsqrt(jnp.maximum(mean_square, NORM_FLOOR))
    attended = (mixed * inverse * gain).astype(BF16)
    return attended, (sigma_query, sigma_key, queries, key_rows, values, weights, mixed, mean_square, inverse)


def replay_kernel(where_ref, x_ref, cot_ref, mask_ref, gain_ref, *refs):
    pieces, (grad_p, att, full) = refs[: len(PIECES)], refs[len(PIECES) :]
    live, here = where_ref[0], where_ref[1]
    place(pieces, here, full)
    slots = x_ref.shape[0] // SEQ_LEN
    for s in range(slots):
        rows = slice(s * SEQ_LEN, (s + 1) * SEQ_LEN)

        @pl.when(s >= live)
        def _():
            grad_p[rows, :] = jnp.zeros((SEQ_LEN, grad_p.shape[1]), BF16)
            att[rows, :] = jnp.zeros((SEQ_LEN, att.shape[1]), BF16)

        @pl.when(s < live)
        def _():
            seq, cot = x_ref[rows, :], cot_ref[rows, :]
            raw = [dot(seq, full[m], 1, 0) for m in range(3)]
            grad_attended = dot(cot, full[3], 1, 0)
            width = att.shape[1]
            for n in range(width // HEAD):
                cols = slice(n * HEAD, (n + 1) * HEAD)
                mask, gain = mask_ref[n], gain_ref[:, cols]
                raw_query, raw_key = raw[0][:, cols], raw[1][:, cols]
                attended, kept = head_forward(raw_query, raw_key, raw[2][:, cols], mask, gain)
                sigma_query, sigma_key, queries, key_rows, values, weights, mixed, mean_square, inverse = kept
                att[rows, cols] = attended
                scaled = grad_attended[:, cols] * gain
                active = jnp.where(mean_square > NORM_FLOOR, 1.0, 0.0)
                mean_dot = jnp.mean(scaled * mixed, axis=-1, keepdims=True)
                grad_mixed = inverse * scaled - mixed * (active * (inverse * inverse * inverse) * mean_dot)
                grad_mixed = grad_mixed.astype(BF16)
                grad_scores = (dot(grad_mixed, values, 1, 1) * mask).astype(BF16)
                grad_values = dot(weights, grad_mixed, 0, 0)
                grad_query = dot(grad_scores, key_rows, 1, 0)
                grad_key = dot(grad_scores, queries, 0, 0)
                grad_query = grad_query * sigma_query * (1.0 + raw_query * (1.0 - sigma_query))
                grad_key = grad_key * sigma_key * (1.0 + raw_key * (1.0 - sigma_key))
                for m, grad in enumerate((grad_query, grad_key, grad_values)):
                    grad_p[rows, m * width + n * HEAD : m * width + (n + 1) * HEAD] = grad.astype(BF16)


def terms_kernel(distances, where_ref, x_ref, cot_ref, grad_p, att, own_ref, other_ref):
    here = where_ref[1]
    rows, width = own_ref.shape[3:]

    def side_terms(side, ref):
        for dx in range(2):
            for block, distance in enumerate(distances):
                owner = (here // (2 * NZ) ^ dx) * NZ + z_owner(here // 2 % NZ, distance, side)
                cols = pl.ds(pl.multiple_of(owner * rows, rows), rows)
                if side == 0:
                    terms = dot(x_ref[:, cols], grad_p[:, : 2 * width], 0, 0).astype(BF16)
                    terms = [terms[:, :width], terms[:, width:]]
                else:
                    terms = [
                        dot(x_ref[:, cols], grad_p[:, 2 * width :], 0, 0).astype(BF16),
                        dot(cot_ref[:, cols], att[...], 0, 0).astype(BF16),
                    ]
                for m, term in enumerate(terms):
                    ref[dx, block, m] = term

    @pl.when(here % 2 == 0)
    def _():
        side_terms(0, own_ref)
        side_terms(1, other_ref)

    @pl.when(here % 2 == 1)
    def _():
        side_terms(1, own_ref)
        side_terms(0, other_ref)


def fresh_kernel(where_ref, x_ref, mask_ref, gain_ref, *refs):
    pieces, (out_ref, full, att) = refs[: len(PIECES)], refs[len(PIECES) :]
    place(pieces, where_ref[1], full)
    seq = x_ref[...]
    raw = [dot(seq, full[m], 1, 0) for m in range(3)]
    width = att.shape[1]
    for n in range(width // HEAD):
        cols = slice(n * HEAD, (n + 1) * HEAD)
        att[:, cols] = head_forward(raw[0][:, cols], raw[1][:, cols], raw[2][:, cols], mask_ref[n], gain_ref[:, cols])[0]
    for first in range(0, full.shape[1], SEQ_LEN):
        cols = slice(first, first + SEQ_LEN)
        out_ref[:, cols] = dot(att[...], full[3, cols, :], 1, 1).astype(BF16)


def kernel_call(body, out_shape, n_vmem, scratch, limit):
    return pl.pallas_call(
        body,
        out_shape=out_shape,
        in_specs=[SMEM] + [VMEM] * n_vmem,
        out_specs=[VMEM] * len(out_shape),
        scratch_shapes=scratch,
        compiler_params=pltpu.CompilerParams(vmem_limit_bytes=limit),
    )


def adam_step(weight, first_moment, second_moment, gradient):
    first_new = BETA_ONE * first_moment + (1.0 - BETA_ONE) * gradient
    second_new = BETA_TWO * second_moment + (1.0 - BETA_TWO) * gradient * gradient
    update = first_new / BIAS_ONE / (jnp.sqrt(second_new / BIAS_TWO) + ADAM_EPS)
    weight_new = weight - LEARN_RATE * (update + WEIGHT_DECAY * weight)
    return (weight_new.astype(BF16), first_new)


def scatter_sum(terms, grads, first_core):
    far, middle, near, last = reversed(SETS)

    def cores(own, from_core):
        both = own.astype(F32) + from_core.astype(F32)
        return both[0], swap(both[1].astype(BF16), X_LO)

    own, other = terms(far, grads)
    from_core = swap(other, CORE)
    next_own, next_other = terms(middle, grads)
    from_core, next_own, next_other, grads = lax.optimization_barrier((from_core, next_own, next_other, grads))
    sums, from_x = cores(own, from_core)
    own, other = next_own, next_other
    from_core = swap(other, CORE)
    next_own, next_other = terms(near, grads)
    from_x, from_core, next_own, next_other, grads = lax.optimization_barrier(
        (from_x, from_core, next_own, next_other, grads)
    )
    passed = z_swap((sums + from_x.astype(F32)).astype(BF16), 3)
    sums, from_x = cores(own, from_core)
    own, other = next_own, next_other
    from_core = swap(other, CORE)
    next_own, next_other = terms(last, grads)
    passed, from_x, from_core, next_own, next_other = lax.optimization_barrier(
        (passed, from_x, from_core, next_own, next_other)
    )
    passed = z_swap((sums + from_x.astype(F32) + passed.astype(F32)).astype(BF16), 2)
    sums, from_x = cores(own, from_core)
    own, from_core = next_own, swap(next_other, CORE)
    passed, from_x, from_core = lax.optimization_barrier((passed, from_x, from_core))
    passed = z_swap((sums + from_x.astype(F32) + passed.astype(F32)).astype(BF16), 1)
    sums, from_x = cores(own, from_core)
    passed, from_x = lax.optimization_barrier((passed, from_x))
    sums = sums + from_x.astype(F32) + passed.astype(F32)
    passed = z_swap(sums[1].astype(BF16), 0)
    chip = sums[0] + passed.astype(F32)
    shard = chip.shape[1] // 2
    low, high = chip[:, :shard], chip[:, shard:]
    mine = jnp.where(first_core, low, high)
    theirs = swap(jnp.where(first_core, high, low).astype(BF16), CORE).astype(F32)
    return jnp.concatenate([jnp.where(first_core, mine, theirs), jnp.where(first_core, theirs, mine)])


def local(
    recorded_input_rows,
    out_cotangent,
    fresh_rows,
    seq_counts,
    decay_logs,
    norm_gain,
    qkv_weight,
    emitted_projection_matrix,
    qkv_first,
    qkv_second,
    out_first,
    out_second,
):
    shard, _, width = qkv_weight.shape
    depth = shard * NH
    ranks = lax.axis_size("tensor")
    rank = lax.axis_index("tensor")
    here = lax.axis_index("helper")
    first_core = here % 2 == 0
    live = lax.dynamic_slice(seq_counts, (here,), (1,))[0]
    where = jnp.stack([live, here]).astype(jnp.int32)
    mask = decay_table(decay_logs)
    gain = norm_gain[None, :]

    def stacked(qkv, out):
        return jnp.concatenate([jnp.transpose(qkv, (1, 0, 2)), out[None]], axis=0)

    old = gather_pieces(stacked(qkv_weight, emitted_projection_matrix).astype(BF16), first_core)
    rows = recorded_input_rows.shape[0]
    grad_p, att = kernel_call(
        replay_kernel,
        [jax.ShapeDtypeStruct((rows, 3 * width), BF16), jax.ShapeDtypeStruct((rows, width), BF16)],
        4 + len(PIECES),
        [pltpu.VMEM((4, depth, width), BF16)],
        44 * 2**20,
    )(where, recorded_input_rows, out_cotangent, mask, gain, *old)

    def terms(distances, grads):
        return kernel_call(
            functools.partial(terms_kernel, distances),
            [jax.ShapeDtypeStruct((2, 2, 2, 2 * shard, width), BF16)] * 2,
            4,
            [],
            32 * 2**20,
        )(where, recorded_input_rows, out_cotangent, *grads)

    grad = scatter_sum(terms, (grad_p, att), first_core)
    new_qkv, qkv_moment = adam_step(qkv_weight, qkv_first, qkv_second, jnp.transpose(grad[:3], (1, 0, 2)))
    new_out, out_moment = adam_step(emitted_projection_matrix, out_first, out_second, grad[3])
    new = gather_pieces(stacked(new_qkv, new_out), first_core)
    part = fresh_rows.shape[0] // ranks
    [partial] = kernel_call(
        fresh_kernel,
        [jax.ShapeDtypeStruct(fresh_rows.shape, BF16)],
        3 + len(PIECES),
        [pltpu.VMEM((4, depth, width), BF16), pltpu.VMEM((fresh_rows.shape[0], width), BF16)],
        40 * 2**20,
    )(where, fresh_rows, mask, gain, *new)
    terms = lax.all_to_all(partial.reshape(ranks, part, depth), "tensor", 0, 0, tiled=True)
    mine = lax.dynamic_slice(fresh_rows, (rank * part, 0), (part, depth)).astype(F32)
    mine = (mine + jnp.sum(terms.astype(F32), axis=0)).astype(BF16)
    fresh_out = lax.all_to_all(jnp.broadcast_to(mine[None], (ranks, part, depth)), "tensor", 0, 0, tiled=True)
    fresh_out = fresh_out.reshape(fresh_rows.shape)
    return (fresh_out, qkv_moment, out_moment)


def solution(mesh):
    return jax.shard_map(
        local,
        mesh=mesh,
        in_specs=(
            P("helper", None),
            P("helper", None),
            P("helper", None),
            P(),
            P("tensor", None),
            P("tensor"),
            P("helper", None, "tensor"),
            P("helper", "tensor"),
            P("helper", None, "tensor"),
            P("helper", None, "tensor"),
            P("helper", "tensor"),
            P("helper", "tensor"),
        ),
        out_specs=(P("helper", None), P("helper", None, "tensor"), P("helper", "tensor")),
        check_vma=False,
    )
```

```python
import functools

import jax
import jax.numpy as jnp
from jax import lax
from jax.experimental import pallas as pl
from jax.experimental.pallas import tpu as pltpu
from jax.sharding import PartitionSpec as P

SEQ_LEN = 256
HEAD = 128

NORM_FLOOR = 1.0
BETA_ONE = 0.9
BETA_TWO = 0.95
ADAM_EPS = 1e-08
LEARN_RATE = 0.005
WEIGHT_DECAY = 0.1
BIAS_ONE = 0.9999734386011124
BIAS_TWO = 0.994079470779666

CORE, X_LO, NZ = 1, 16, 8
SETS = ((0, 1), (-1, -2), (2, 3), (-3, -4))
NH = 32
F32, BF16 = jnp.float32, jnp.bfloat16
VMEM = pl.BlockSpec(memory_space=pltpu.VMEM)
SMEM = pl.BlockSpec(memory_space=pltpu.SMEM)


def swap(block, distance):
    return lax.ppermute(block, "helper", [(i ^ distance, i) for i in range(NH)])


def z_swap(block, step):
    def partner(i):
        x, z, c = i // (2 * NZ), i // 2 % NZ, i % 2
        return (x * NZ + (z + (1 if (z + c + step) % 2 == 0 else -1)) % NZ) * 2 + c

    return lax.ppermute(block, "helper", [(partner(i), i) for i in range(NH)])


def z_owner(z, distance, side):
    sign = (1 - 2 * (z % 2)) * (1 - 2 * side)
    return (z + sign * distance + NZ) % NZ


def decay_table(decay_logs):
    length = decay_logs.shape[1]
    later = (jnp.arange(length)[:, None] >= jnp.arange(length)[None, :])[None]
    running = jnp.sum(jnp.where(later, decay_logs[:, None, :], 0.0), axis=2)
    spread_factor = running[:, :, None] - running[:, None, :]
    return jnp.where(later, jnp.exp(jnp.where(later, spread_factor, 0.0)), 0.0)


def dot(a, b, ca, cb):
    return lax.dot_general(a, b, (((ca,), (cb,)), ((), ())), preferred_element_type=F32)


def side_of(parts, first_core, own):
    return jnp.where(first_core == own, parts[:2], parts[2:])


def gather_pieces(piece, first_core, beside=()):
    mine, theirs = side_of(piece, first_core, True), swap(side_of(piece, first_core, False), CORE)
    rows = [jnp.where(first_core, mine, theirs), jnp.where(first_core, theirs, mine)]
    block = jnp.concatenate(rows, axis=1)[None]
    got, other_x = [block], []
    for step in range(4):
        other_x.append(swap(got[-1], X_LO))
        now = z_swap(block, step)
        if step == 2:
            now, other_x[-1], beside = lax.optimization_barrier((now, other_x[-1], beside))
        else:
            now, other_x[-1] = lax.optimization_barrier((now, other_x[-1]))
        got.append(now)
        block = now if step else jnp.concatenate([block, now])
    got = got + other_x + [swap(got[-1], X_LO)]
    return beside, got + [swap(block, CORE) for block in got]


PIECES = [(c, x, z) for c in range(2) for x in range(2) for z in (SETS[0][:1], SETS[0][1:], *SETS[1:])]


def place(pieces, here, full):
    z = here // 2 % NZ
    parts, rows = pieces[0].shape[1:3]
    for (c, x, distances), piece in zip(PIECES, pieces):
        side = here % 2 ^ c
        for block, distance in enumerate(distances):
            owner = (here // (2 * NZ) ^ x) * NZ + z_owner(z, distance, side)
            start = pl.multiple_of(owner * rows, rows)
            for m in range(parts):
                full[side * parts + m, pl.ds(start, rows), :] = piece[block, m]


def head_forward(raw_query, raw_key, raw_value, mask, gain):
    sigma_query, sigma_key = jax.nn.sigmoid(raw_query), jax.nn.sigmoid(raw_key)
    queries = (raw_query * sigma_query).astype(BF16)
    key_rows = (raw_key * sigma_key).astype(BF16)
    values = raw_value.astype(BF16)
    weights = (dot(queries, key_rows, 1, 1) * mask).astype(BF16)
    mixed = dot(weights, values, 1, 0)
    mean_square = jnp.mean(mixed * mixed, axis=-1, keepdims=True)
    inverse = lax.rsqrt(jnp.maximum(mean_square, NORM_FLOOR))
    attended = (mixed * inverse * gain).astype(BF16)
    return attended, (sigma_query, sigma_key, queries, key_rows, values, weights, mixed, mean_square, inverse)


def replay_kernel(where_ref, x_ref, cot_ref, mask_ref, gain_ref, *refs):
    pieces, (grad_p, att, full, x_held, cot_held, sems) = refs[: len(PIECES)], refs[len(PIECES) :]
    live, here = where_ref[0], where_ref[1]
    slots = x_ref.shape[0] // SEQ_LEN

    def copies(s):
        rows = slice(s * SEQ_LEN, (s + 1) * SEQ_LEN)
        pairs = ((x_ref, x_held), (cot_ref, cot_held))
        return [
            pltpu.make_async_copy(source.at[rows, :], held.at[rows, :], sems.at[i, s])
            for i, (source, held) in enumerate(pairs)
        ]

    for s in range(slots):

        @pl.when(s < live)
        def _():
            for copy in copies(s):
                copy.start()

    place(pieces, here, full)
    for s in range(slots):
        rows = slice(s * SEQ_LEN, (s + 1) * SEQ_LEN)

        @pl.when(s >= live)
        def _():
            grad_p[rows, :] = jnp.zeros((SEQ_LEN, grad_p.shape[1]), BF16)
            att[rows, :] = jnp.zeros((SEQ_LEN, att.shape[1]), BF16)

        @pl.when(s < live)
        def _():
            for copy in copies(s):
                copy.wait()
            seq, cot = x_held[rows, :], cot_held[rows, :]
            raw = [dot(seq, full[m], 1, 0) for m in range(3)]
            grad_attended = dot(cot, full[3], 1, 0)
            width = att.shape[1]
            for n in range(width // HEAD):
                cols = slice(n * HEAD, (n + 1) * HEAD)
                mask, gain = mask_ref[n], gain_ref[:, cols]
                raw_query, raw_key = raw[0][:, cols], raw[1][:, cols]
                attended, kept = head_forward(raw_query, raw_key, raw[2][:, cols], mask, gain)
                sigma_query, sigma_key, queries, key_rows, values, weights, mixed, mean_square, inverse = kept
                att[rows, cols] = attended
                scaled = grad_attended[:, cols] * gain
                active = jnp.where(mean_square > NORM_FLOOR, 1.0, 0.0)
                mean_dot = jnp.mean(scaled * mixed, axis=-1, keepdims=True)
                grad_mixed = inverse * scaled - mixed * (active * (inverse * inverse * inverse) * mean_dot)
                grad_mixed = grad_mixed.astype(BF16)
                grad_scores = (dot(grad_mixed, values, 1, 1) * mask).astype(BF16)
                grad_values = dot(weights, grad_mixed, 0, 0)
                grad_query = dot(grad_scores, key_rows, 1, 0)
                grad_key = dot(grad_scores, queries, 0, 0)
                grad_query = grad_query * sigma_query * (1.0 + raw_query * (1.0 - sigma_query))
                grad_key = grad_key * sigma_key * (1.0 + raw_key * (1.0 - sigma_key))
                for m, grad in enumerate((grad_query, grad_key, grad_values)):
                    grad_p[rows, m * width + n * HEAD : m * width + (n + 1) * HEAD] = grad.astype(BF16)


def terms_kernel(distances, where_ref, x_ref, cot_ref, grad_p, att, own_ref, other_ref):
    here = where_ref[1]
    rows, width = own_ref.shape[3:]

    def side_terms(side, ref):
        for dx in range(2):
            for block, distance in enumerate(distances):
                owner = (here // (2 * NZ) ^ dx) * NZ + z_owner(here // 2 % NZ, distance, side)
                cols = pl.ds(pl.multiple_of(owner * rows, rows), rows)
                if side == 0:
                    terms = dot(x_ref[:, cols], grad_p[:, : 2 * width], 0, 0).astype(BF16)
                    terms = [terms[:, :width], terms[:, width:]]
                else:
                    terms = [
                        dot(x_ref[:, cols], grad_p[:, 2 * width :], 0, 0).astype(BF16),
                        dot(cot_ref[:, cols], att[...], 0, 0).astype(BF16),
                    ]
                for m, term in enumerate(terms):
                    ref[dx, block, m] = term

    @pl.when(here % 2 == 0)
    def _():
        side_terms(0, own_ref)
        side_terms(1, other_ref)

    @pl.when(here % 2 == 1)
    def _():
        side_terms(1, own_ref)
        side_terms(0, other_ref)


def fresh_kernel(where_ref, x_ref, mask_ref, gain_ref, *refs):
    pieces, (out_ref, full, att) = refs[: len(PIECES)], refs[len(PIECES) :]
    place(pieces, where_ref[1], full)
    seq = x_ref[...]
    raw = [dot(seq, full[m], 1, 0) for m in range(3)]
    width = att.shape[1]
    for n in range(width // HEAD):
        cols = slice(n * HEAD, (n + 1) * HEAD)
        att[:, cols] = head_forward(raw[0][:, cols], raw[1][:, cols], raw[2][:, cols], mask_ref[n], gain_ref[:, cols])[0]
    for first in range(0, full.shape[1], SEQ_LEN):
        cols = slice(first, first + SEQ_LEN)
        out_ref[:, cols] = dot(att[...], full[3, cols, :], 1, 1).astype(BF16)


def kernel_call(body, out_shape, n_vmem, scratch, limit, n_hbm=0):
    return pl.pallas_call(
        body,
        out_shape=out_shape,
        in_specs=[SMEM] + [pl.BlockSpec(memory_space=pltpu.HBM)] * n_hbm + [VMEM] * n_vmem,
        out_specs=[VMEM] * len(out_shape),
        scratch_shapes=scratch,
        compiler_params=pltpu.CompilerParams(vmem_limit_bytes=limit),
    )


def adam_step(weight, first_moment, second_moment, gradient):
    first_new = BETA_ONE * first_moment + (1.0 - BETA_ONE) * gradient
    second_new = BETA_TWO * second_moment + (1.0 - BETA_TWO) * gradient * gradient
    update = first_new / BIAS_ONE / (jnp.sqrt(second_new / BIAS_TWO) + ADAM_EPS)
    weight_new = weight - LEARN_RATE * (update + WEIGHT_DECAY * weight)
    return (weight_new.astype(BF16), first_new)


def scatter_sum(terms, grads, first_core):
    far, middle, near, last = reversed(SETS)

    def cores(own, from_core):
        both = own.astype(F32) + from_core.astype(F32)
        return both[0], swap(both[1].astype(BF16), X_LO)

    own, other = terms(far, grads)
    from_core = swap(other, CORE)
    next_own, next_other = terms(middle, grads)
    from_core, next_own, next_other, grads = lax.optimization_barrier((from_core, next_own, next_other, grads))
    sums, from_x = cores(own, from_core)
    own, other = next_own, next_other
    from_core = swap(other, CORE)
    next_own, next_other = terms(near, grads)
    from_x, from_core, next_own, next_other, grads = lax.optimization_barrier(
        (from_x, from_core, next_own, next_other, grads)
    )
    passed = z_swap((sums + from_x.astype(F32)).astype(BF16), 3)
    sums, from_x = cores(own, from_core)
    own, other = next_own, next_other
    from_core = swap(other, CORE)
    next_own, next_other = terms(last, grads)
    passed, from_x, from_core, next_own, next_other = lax.optimization_barrier(
        (passed, from_x, from_core, next_own, next_other)
    )
    passed = z_swap((sums + from_x.astype(F32) + passed.astype(F32)).astype(BF16), 2)
    sums, from_x = cores(own, from_core)
    own, from_core = next_own, swap(next_other, CORE)
    passed, from_x, from_core = lax.optimization_barrier((passed, from_x, from_core))
    passed = z_swap((sums + from_x.astype(F32) + passed.astype(F32)).astype(BF16), 1)
    sums, from_x = cores(own, from_core)
    passed, from_x = lax.optimization_barrier((passed, from_x))
    sums = sums + from_x.astype(F32) + passed.astype(F32)
    passed = z_swap(sums[1].astype(BF16), 0)
    chip = sums[0] + passed.astype(F32)
    shard = chip.shape[1] // 2
    low, high = chip[:, :shard], chip[:, shard:]
    mine = jnp.where(first_core, low, high)
    theirs = swap(jnp.where(first_core, high, low).astype(BF16), CORE).astype(F32)
    return jnp.concatenate([jnp.where(first_core, mine, theirs), jnp.where(first_core, theirs, mine)])


def local(
    recorded_input_rows,
    out_cotangent,
    fresh_rows,
    seq_counts,
    decay_logs,
    norm_gain,
    qkv_weight,
    emitted_projection_matrix,
    qkv_first,
    qkv_second,
    out_first,
    out_second,
):
    shard, _, width = qkv_weight.shape
    depth = shard * NH
    ranks = lax.axis_size("tensor")
    rank = lax.axis_index("tensor")
    here = lax.axis_index("helper")
    first_core = here % 2 == 0
    live = lax.dynamic_slice(seq_counts, (here,), (1,))[0]
    where = jnp.stack([live, here]).astype(jnp.int32)
    mask = decay_table(decay_logs)
    gain = norm_gain[None, :]

    def stacked(qkv, out):
        return jnp.concatenate([jnp.transpose(qkv, (1, 0, 2)), out[None]], axis=0)

    (where, gain, mask), old = gather_pieces(
        stacked(qkv_weight, emitted_projection_matrix).astype(BF16), first_core, (where, gain, mask)
    )
    rows = recorded_input_rows.shape[0]
    grad_p, att = kernel_call(
        replay_kernel,
        [jax.ShapeDtypeStruct((rows, 3 * width), BF16), jax.ShapeDtypeStruct((rows, width), BF16)],
        2 + len(PIECES),
        [
            pltpu.VMEM((4, depth, width), BF16),
            pltpu.VMEM((rows, depth), BF16),
            pltpu.VMEM((rows, depth), BF16),
            pltpu.SemaphoreType.DMA((2, rows // SEQ_LEN)),
        ],
        44 * 2**20,
        2,
    )(where, recorded_input_rows, out_cotangent, mask, gain, *old)

    def terms(distances, grads):
        return kernel_call(
            functools.partial(terms_kernel, distances),
            [jax.ShapeDtypeStruct((2, 2, 2, 2 * shard, width), BF16)] * 2,
            4,
            [],
            32 * 2**20,
        )(where, recorded_input_rows, out_cotangent, *grads)

    grad = scatter_sum(terms, (grad_p, att), first_core)
    new_qkv, qkv_moment = adam_step(qkv_weight, qkv_first, qkv_second, jnp.transpose(grad[:3], (1, 0, 2)))
    new_out, out_moment = adam_step(emitted_projection_matrix, out_first, out_second, grad[3])
    _, new = gather_pieces(stacked(new_qkv, new_out), first_core)
    part = fresh_rows.shape[0] // ranks
    [partial] = kernel_call(
        fresh_kernel,
        [jax.ShapeDtypeStruct(fresh_rows.shape, BF16)],
        3 + len(PIECES),
        [pltpu.VMEM((4, depth, width), BF16), pltpu.VMEM((fresh_rows.shape[0], width), BF16)],
        40 * 2**20,
    )(where, fresh_rows, mask, gain, *new)
    terms = lax.all_to_all(partial.reshape(ranks, part, depth), "tensor", 0, 0, tiled=True)
    mine = lax.dynamic_slice(fresh_rows, (rank * part, 0), (part, depth)).astype(F32)
    mine = (mine + jnp.sum(terms.astype(F32), axis=0)).astype(BF16)
    fresh_out = lax.all_to_all(jnp.broadcast_to(mine[None], (ranks, part, depth)), "tensor", 0, 0, tiled=True)
    fresh_out = fresh_out.reshape(fresh_rows.shape)
    return (fresh_out, qkv_moment, out_moment)


def solution(mesh):
    return jax.shard_map(
        local,
        mesh=mesh,
        in_specs=(
            P("helper", None),
            P("helper", None),
            P("helper", None),
            P(),
            P("tensor", None),
            P("tensor"),
            P("helper", None, "tensor"),
            P("helper", "tensor"),
            P("helper", None, "tensor"),
            P("helper", None, "tensor"),
            P("helper", "tensor"),
            P("helper", "tensor"),
        ),
        out_specs=(P("helper", None), P("helper", None, "tensor"), P("helper", "tensor")),
        check_vma=False,
    )
```

```python
import functools

import jax
import jax.numpy as jnp
from jax import lax
from jax.experimental import pallas as pl
from jax.experimental.pallas import tpu as pltpu
from jax.sharding import PartitionSpec as P

SEQ_LEN = 256
HEAD = 128

NORM_FLOOR = 1.0
BETA_ONE = 0.9
BETA_TWO = 0.95
ADAM_EPS = 1e-08
LEARN_RATE = 0.005
WEIGHT_DECAY = 0.1
BIAS_ONE = 0.9999734386011124
BIAS_TWO = 0.994079470779666

CORE, X_LO, NZ = 1, 16, 8
SETS = ((0, 1), (-1, -2), (2, 3), (-3, -4))
NH = 32
F32, BF16 = jnp.float32, jnp.bfloat16
VMEM = pl.BlockSpec(memory_space=pltpu.VMEM)
SMEM = pl.BlockSpec(memory_space=pltpu.SMEM)


def swap(block, distance):
    return lax.ppermute(block, "helper", [(i ^ distance, i) for i in range(NH)])


def z_swap(block, step):
    def partner(i):
        x, z, c = i // (2 * NZ), i // 2 % NZ, i % 2
        return (x * NZ + (z + (1 if (z + c + step) % 2 == 0 else -1)) % NZ) * 2 + c

    return lax.ppermute(block, "helper", [(partner(i), i) for i in range(NH)])


def z_owner(z, distance, side):
    sign = (1 - 2 * (z % 2)) * (1 - 2 * side)
    return (z + sign * distance + NZ) % NZ


def decay_table(decay_logs):
    length = decay_logs.shape[1]
    later = (jnp.arange(length)[:, None] >= jnp.arange(length)[None, :])[None]
    running = jnp.sum(jnp.where(later, decay_logs[:, None, :], 0.0), axis=2)
    spread_factor = running[:, :, None] - running[:, None, :]
    return jnp.where(later, jnp.exp(jnp.where(later, spread_factor, 0.0)), 0.0)


def dot(a, b, ca, cb):
    return lax.dot_general(a, b, (((ca,), (cb,)), ((), ())), preferred_element_type=F32)


def chip_rows(parts, first_core):
    low, high = parts[..., :2, :, :], parts[..., 2:, :, :]
    mine = jnp.where(first_core, low, high)
    theirs = swap(jnp.where(first_core, high, low), CORE)
    rows = [jnp.where(first_core, mine, theirs), jnp.where(first_core, theirs, mine)]
    return jnp.concatenate(rows, axis=-2)


def own_rows(parts, first_core):
    shard = parts.shape[1] // 2
    low, high = parts[:, :shard], parts[:, shard:]
    mine = jnp.where(first_core, low, high)
    theirs = swap(jnp.where(first_core, high, low), CORE)
    return jnp.concatenate([jnp.where(first_core, mine, theirs), jnp.where(first_core, theirs, mine)])


def gather_pieces(block, beside=()):
    block = block[None]
    got, other_x = [block], []
    for step in range(4):
        other_x.append(swap(got[-1], X_LO))
        now = z_swap(block, step)
        if step == 2:
            now, other_x[-1], beside = lax.optimization_barrier((now, other_x[-1], beside))
        else:
            now, other_x[-1] = lax.optimization_barrier((now, other_x[-1]))
        got.append(now)
        block = now if step else jnp.concatenate([block, now])
    got = got + other_x + [swap(got[-1], X_LO)]
    return beside, got + [swap(block, CORE) for block in got]


PIECES = [(c, x, z) for c in range(2) for x in range(2) for z in (SETS[0][:1], SETS[0][1:], *SETS[1:])]


def place(pieces, here, full):
    z = here // 2 % NZ
    parts, rows = pieces[0].shape[1:3]
    for (c, x, distances), piece in zip(PIECES, pieces):
        side = here % 2 ^ c
        for block, distance in enumerate(distances):
            owner = (here // (2 * NZ) ^ x) * NZ + z_owner(z, distance, side)
            start = pl.multiple_of(owner * rows, rows)
            for m in range(parts):
                full[side * parts + m, pl.ds(start, rows), :] = piece[block, m]


def head_forward(raw_query, raw_key, raw_value, mask, gain):
    sigma_query, sigma_key = jax.nn.sigmoid(raw_query), jax.nn.sigmoid(raw_key)
    queries = (raw_query * sigma_query).astype(BF16)
    key_rows = (raw_key * sigma_key).astype(BF16)
    values = raw_value.astype(BF16)
    weights = (dot(queries, key_rows, 1, 1) * mask).astype(BF16)
    mixed = dot(weights, values, 1, 0)
    mean_square = jnp.mean(mixed * mixed, axis=-1, keepdims=True)
    inverse = lax.rsqrt(jnp.maximum(mean_square, NORM_FLOOR))
    attended = (mixed * inverse * gain).astype(BF16)
    return attended, (sigma_query, sigma_key, queries, key_rows, values, weights, mixed, mean_square, inverse)


def replay_kernel(where_ref, x_ref, cot_ref, mask_ref, gain_ref, *refs):
    pieces, (grad_p, att, full, x_held, cot_held, sems) = refs[: len(PIECES)], refs[len(PIECES) :]
    live, here = where_ref[0], where_ref[1]
    slots = x_ref.shape[0] // SEQ_LEN

    def copies(s):
        rows = slice(s * SEQ_LEN, (s + 1) * SEQ_LEN)
        pairs = ((x_ref, x_held), (cot_ref, cot_held))
        return [
            pltpu.make_async_copy(source.at[rows, :], held.at[rows, :], sems.at[i, s])
            for i, (source, held) in enumerate(pairs)
        ]

    for s in range(slots):

        @pl.when(s < live)
        def _():
            for copy in copies(s):
                copy.start()

    place(pieces, here, full)
    for s in range(slots):
        rows = slice(s * SEQ_LEN, (s + 1) * SEQ_LEN)

        @pl.when(s >= live)
        def _():
            grad_p[rows, :] = jnp.zeros((SEQ_LEN, grad_p.shape[1]), BF16)
            att[rows, :] = jnp.zeros((SEQ_LEN, att.shape[1]), BF16)

        @pl.when(s < live)
        def _():
            for copy in copies(s):
                copy.wait()
            seq, cot = x_held[rows, :], cot_held[rows, :]
            raw = [dot(seq, full[m], 1, 0) for m in range(3)]
            grad_attended = dot(cot, full[3], 1, 0)
            width = att.shape[1]
            for n in range(width // HEAD):
                cols = slice(n * HEAD, (n + 1) * HEAD)
                mask, gain = mask_ref[n], gain_ref[:, cols]
                raw_query, raw_key = raw[0][:, cols], raw[1][:, cols]
                attended, kept = head_forward(raw_query, raw_key, raw[2][:, cols], mask, gain)
                sigma_query, sigma_key, queries, key_rows, values, weights, mixed, mean_square, inverse = kept
                att[rows, cols] = attended
                scaled = grad_attended[:, cols] * gain
                active = jnp.where(mean_square > NORM_FLOOR, 1.0, 0.0)
                mean_dot = jnp.mean(scaled * mixed, axis=-1, keepdims=True)
                grad_mixed = inverse * scaled - mixed * (active * (inverse * inverse * inverse) * mean_dot)
                grad_mixed = grad_mixed.astype(BF16)
                grad_scores = (dot(grad_mixed, values, 1, 1) * mask).astype(BF16)
                grad_values = dot(weights, grad_mixed, 0, 0)
                grad_query = dot(grad_scores, key_rows, 1, 0)
                grad_key = dot(grad_scores, queries, 0, 0)
                grad_query = grad_query * sigma_query * (1.0 + raw_query * (1.0 - sigma_query))
                grad_key = grad_key * sigma_key * (1.0 + raw_key * (1.0 - sigma_key))
                for m, grad in enumerate((grad_query, grad_key, grad_values)):
                    grad_p[rows, m * width + n * HEAD : m * width + (n + 1) * HEAD] = grad.astype(BF16)


def terms_kernel(distances, where_ref, x_ref, cot_ref, grad_p, att, own_ref, other_ref):
    here = where_ref[1]
    rows, width = own_ref.shape[3:]

    def side_terms(side, ref):
        for dx in range(2):
            for block, distance in enumerate(distances):
                owner = (here // (2 * NZ) ^ dx) * NZ + z_owner(here // 2 % NZ, distance, side)
                cols = pl.ds(pl.multiple_of(owner * rows, rows), rows)
                if side == 0:
                    terms = dot(x_ref[:, cols], grad_p[:, : 2 * width], 0, 0).astype(BF16)
                    terms = [terms[:, :width], terms[:, width:]]
                else:
                    terms = [
                        dot(x_ref[:, cols], grad_p[:, 2 * width :], 0, 0).astype(BF16),
                        dot(cot_ref[:, cols], att[...], 0, 0).astype(BF16),
                    ]
                for m, term in enumerate(terms):
                    ref[dx, block, m] = term

    @pl.when(here % 2 == 0)
    def _():
        side_terms(0, own_ref)
        side_terms(1, other_ref)

    @pl.when(here % 2 == 1)
    def _():
        side_terms(1, own_ref)
        side_terms(0, other_ref)


def fresh_kernel(where_ref, x_ref, mask_ref, gain_ref, *refs):
    pieces, (out_ref, full, att) = refs[: len(PIECES)], refs[len(PIECES) :]
    place(pieces, where_ref[1], full)
    seq = x_ref[...]
    raw = [dot(seq, full[m], 1, 0) for m in range(3)]
    width = att.shape[1]
    for n in range(width // HEAD):
        cols = slice(n * HEAD, (n + 1) * HEAD)
        att[:, cols] = head_forward(raw[0][:, cols], raw[1][:, cols], raw[2][:, cols], mask_ref[n], gain_ref[:, cols])[0]
    for first in range(0, full.shape[1], SEQ_LEN):
        cols = slice(first, first + SEQ_LEN)
        out_ref[:, cols] = dot(att[...], full[3, cols, :], 1, 1).astype(BF16)


def kernel_call(body, out_shape, n_vmem, scratch, limit, n_hbm=0):
    return pl.pallas_call(
        body,
        out_shape=out_shape,
        in_specs=[SMEM] + [pl.BlockSpec(memory_space=pltpu.HBM)] * n_hbm + [VMEM] * n_vmem,
        out_specs=[VMEM] * len(out_shape),
        scratch_shapes=scratch,
        compiler_params=pltpu.CompilerParams(vmem_limit_bytes=limit),
    )


def adam_step(weight, first_moment, second_moment, gradient):
    first_new = BETA_ONE * first_moment + (1.0 - BETA_ONE) * gradient
    second_new = BETA_TWO * second_moment + (1.0 - BETA_TWO) * gradient * gradient
    update = first_new / BIAS_ONE / (jnp.sqrt(second_new / BIAS_TWO) + ADAM_EPS)
    weight_new = weight - LEARN_RATE * (update + WEIGHT_DECAY * weight)
    return (weight_new.astype(BF16), first_new)


def scatter_sum(terms, grads):
    far, middle, near, last = reversed(SETS)

    def cores(own, from_core):
        both = own.astype(F32) + from_core.astype(F32)
        return both[0], swap(both[1].astype(BF16), X_LO)

    own, other = terms(far, grads)
    from_core = swap(other, CORE)
    next_own, next_other = terms(middle, grads)
    from_core, next_own, next_other, grads = lax.optimization_barrier((from_core, next_own, next_other, grads))
    sums, from_x = cores(own, from_core)
    own, other = next_own, next_other
    from_core = swap(other, CORE)
    next_own, next_other = terms(near, grads)
    from_x, from_core, next_own, next_other, grads = lax.optimization_barrier(
        (from_x, from_core, next_own, next_other, grads)
    )
    passed = z_swap((sums + from_x.astype(F32)).astype(BF16), 3)
    sums, from_x = cores(own, from_core)
    own, other = next_own, next_other
    from_core = swap(other, CORE)
    next_own, next_other = terms(last, grads)
    passed, from_x, from_core, next_own, next_other = lax.optimization_barrier(
        (passed, from_x, from_core, next_own, next_other)
    )
    passed = z_swap((sums + from_x.astype(F32) + passed.astype(F32)).astype(BF16), 2)
    sums, from_x = cores(own, from_core)
    own, from_core = next_own, swap(next_other, CORE)
    passed, from_x, from_core = lax.optimization_barrier((passed, from_x, from_core))
    passed = z_swap((sums + from_x.astype(F32) + passed.astype(F32)).astype(BF16), 1)
    sums, from_x = cores(own, from_core)
    passed, from_x = lax.optimization_barrier((passed, from_x))
    sums = sums + from_x.astype(F32) + passed.astype(F32)
    passed = z_swap(sums[1].astype(BF16), 0)
    return sums[0] + passed.astype(F32)


def local(
    recorded_input_rows,
    out_cotangent,
    fresh_rows,
    seq_counts,
    decay_logs,
    norm_gain,
    qkv_weight,
    emitted_projection_matrix,
    qkv_first,
    qkv_second,
    out_first,
    out_second,
):
    shard, _, width = qkv_weight.shape
    depth = shard * NH
    ranks = lax.axis_size("tensor")
    rank = lax.axis_index("tensor")
    here = lax.axis_index("helper")
    first_core = here % 2 == 0
    live = lax.dynamic_slice(seq_counts, (here,), (1,))[0]
    where = jnp.stack([live, here]).astype(jnp.int32)
    mask = decay_table(decay_logs)
    gain = norm_gain[None, :]

    def stacked(qkv, out):
        return jnp.concatenate([jnp.transpose(qkv, (1, 0, 2)), out[None]], axis=0)

    weight = stacked(qkv_weight, emitted_projection_matrix)
    states = jnp.stack([weight, stacked(qkv_first, out_first), stacked(qkv_second, out_second)])
    block = chip_rows(weight.astype(BF16), first_core)
    block, states = lax.optimization_barrier((block, states))
    beside = (where, gain, mask, chip_rows(states, first_core))
    (where, gain, mask, states), old = gather_pieces(block, beside)
    rows = recorded_input_rows.shape[0]
    grad_p, att = kernel_call(
        replay_kernel,
        [jax.ShapeDtypeStruct((rows, 3 * width), BF16), jax.ShapeDtypeStruct((rows, width), BF16)],
        2 + len(PIECES),
        [
            pltpu.VMEM((4, depth, width), BF16),
            pltpu.VMEM((rows, depth), BF16),
            pltpu.VMEM((rows, depth), BF16),
            pltpu.SemaphoreType.DMA((2, rows // SEQ_LEN)),
        ],
        44 * 2**20,
        2,
    )(where, recorded_input_rows, out_cotangent, mask, gain, *old)

    def terms(distances, grads):
        return kernel_call(
            functools.partial(terms_kernel, distances),
            [jax.ShapeDtypeStruct((2, 2, 2, 2 * shard, width), BF16)] * 2,
            4,
            [],
            32 * 2**20,
        )(where, recorded_input_rows, out_cotangent, *grads)

    grad = scatter_sum(terms, (grad_p, att))
    new_block, moment = adam_step(states[0], states[1], states[2], grad)
    _, new = gather_pieces(new_block)
    moment, new[-1] = lax.optimization_barrier((moment, new[-1]))
    moment = own_rows(moment, first_core)
    qkv_moment, out_moment = jnp.transpose(moment[:3], (1, 0, 2)), moment[3]
    part = fresh_rows.shape[0] // ranks
    [partial] = kernel_call(
        fresh_kernel,
        [jax.ShapeDtypeStruct(fresh_rows.shape, BF16)],
        3 + len(PIECES),
        [pltpu.VMEM((4, depth, width), BF16), pltpu.VMEM((fresh_rows.shape[0], width), BF16)],
        40 * 2**20,
    )(where, fresh_rows, mask, gain, *new)
    terms = lax.all_to_all(partial.reshape(ranks, part, depth), "tensor", 0, 0, tiled=True)
    mine = lax.dynamic_slice(fresh_rows, (rank * part, 0), (part, depth)).astype(F32)
    mine = (mine + jnp.sum(terms.astype(F32), axis=0)).astype(BF16)
    fresh_out = lax.all_to_all(jnp.broadcast_to(mine[None], (ranks, part, depth)), "tensor", 0, 0, tiled=True)
    fresh_out = fresh_out.reshape(fresh_rows.shape)
    return (fresh_out, qkv_moment, out_moment)


def solution(mesh):
    return jax.shard_map(
        local,
        mesh=mesh,
        in_specs=(
            P("helper", None),
            P("helper", None),
            P("helper", None),
            P(),
            P("tensor", None),
            P("tensor"),
            P("helper", None, "tensor"),
            P("helper", "tensor"),
            P("helper", None, "tensor"),
            P("helper", None, "tensor"),
            P("helper", "tensor"),
            P("helper", "tensor"),
        ),
        out_specs=(P("helper", None), P("helper", None, "tensor"), P("helper", "tensor")),
        check_vma=False,
    )
```
